32 devices in a mesh: groups: 2 (over y), expert: 4 (over z), helper: 4 (over x, core).
Axes of the slice: x: 2, y: 2, z: 4, core: 2. Of those that a mesh axis runs over, the one named last changes fastest.
Arguments:
- tokens: bfloat16 [256, 3584], P(('groups', 'expert'), 'helper'), parts along dimension 0, may hold values from -6 to 6
- up_weight: bfloat16 [64, 3584, 1024], P('expert', None, 'helper'), may hold values from -0.09375 to 0.09375
- down_weight: bfloat16 [64, 1024, 3584], P('expert', 'helper'), may hold values from -0.1875 to 0.1875
- expert_ids: int32 [256, 8], P(('groups', 'expert')), parts along dimension 0, may hold values from 0 to 63, all different within a row; in each aligned block of 32 rows (0 to 31, 32 to 63, ...) at most 8 rows name the same one
- route_scores: float32 [256, 8], P(('groups', 'expert')), parts along dimension 0, may hold values from 0.1 to 1
Outputs:
- layer_out: bfloat16 [256, 3584], P(('groups', 'expert'), 'helper'), parts along dimension 0
The draws below stay inside these ranges and needn't reach their ends.
There are 2 independent parts, one for each index of `groups`. The reference program is written for one: setup_inputs(seed, part) draws one part's arguments, and reference() takes and returns one part's arrays. A program takes and returns all parts, laid end to end along the dimension named above; an argument that names none is the same for every part. Nothing has to cross between parts.
Inputs may be any that keep to these rules, and one draw needn't show every extreme that they name: `expert_ids`: each token names 8 different experts. In each aligned block of 32 tokens (the tokens of one index of expert) no expert is named by more than 8 tokens, a bound that some block reaches.
All inputs are finite; a program needn't handle non-finite values.
Results may differ from the reference program's by a relative error of at most 0.012.
Values may be sent and summed in bfloat16 or wider, within the bound.
A program may use at most 192 MiB of HBM per device.

```python
import math
import jax
import jax.numpy as jnp
import numpy as np
from jax import lax

D = 3584
FF = 1024
EXPERTS = 64
TOP = 8
TOK_EXP = 32
TOKENS = 128
CAP = 8
FF_DEV = 256
N_EXPERT = 4
N_HELPER = 4


def block_scale(rng, shape, split, least, top_value):
    loudness, own = 1.0, jax.random.fold_in(rng, 6)
    for dim, blocks in split:
        steps = jnp.exp(jax.random.uniform(jax.random.fold_in(own, dim), (blocks,), jnp.float32, least / len(split), top_value / len(split)))
        loudness = loudness * jnp.repeat(steps, shape[dim] // blocks).reshape([-1 if axis == dim else 1 for axis in range(len(shape))])
    return loudness


def deal_out(key, own, number, rows, count, top, limit, slope):
    ranking = jax.random.permutation(key, count)
    heavy_load, common = shares(count, rows * top, limit, slope, True), shares(count, rows * top, limit, slope, False)
    places = jnp.arange(count)

    def named(lengths, offset_by):
        used = int((lengths > 0).sum())
        fixed = max(1, used // 4)
        moved = fixed + (places - fixed + offset_by * (used - fixed)) % max(1, count - fixed)
        return jnp.zeros((count,), jnp.int32).at[ranking[jnp.where(places < fixed, places, moved)]].set(jnp.asarray(lengths, jnp.int32))

    lengths = jnp.where(number % 4 == 0, named(heavy_load, number // 4), named(common, number - number // 4 - 1))
    mixed = jax.random.permutation(jax.random.fold_in(own, 3), count)
    source_of, sink = mixed[0:count // 2 * 2:2], mixed[1:count // 2 * 2:2]
    slack = jnp.minimum(lengths[source_of] - 1, limit - lengths[sink]) // 2
    slack = jnp.where((source_of == ranking[0]) | (sink == ranking[0]) | (lengths[sink] == 0), 0, jnp.maximum(slack, 0))
    moved = jax.random.randint(jax.random.fold_in(own, 4), (count // 2,), 0, 1 << 20) % (slack + 1)
    lengths = lengths.at[source_of].add(-moved).at[sink].add(moved)
    members = jnp.searchsorted(jnp.cumsum(lengths), jnp.arange(rows * top), side="right").astype(jnp.int32)
    grid = members.reshape(top, rows).T
    grid = grid[jax.random.permutation(jax.random.fold_in(own, 1), rows)]
    offset_by = jax.random.randint(jax.random.fold_in(own, 2), (rows, 1), 0, top)
    return jnp.take_along_axis(grid, (jnp.arange(top)[None, :] + offset_by) % top, axis=1)


def shares(amount, total, most, slope, full):
    portions = [(1 << 20) // math.isqrt(rank ** slope) + 1 for rank in range(1, amount + 1)]
    largest = most if full else min(most, max(-(-total // amount), total * portions[0] // sum(portions)))
    least = 1 if total - largest >= amount - 1 else 0
    holding, surplus = [largest] + [least] * (amount - 1), total - largest - least * (amount - 1)
    while surplus > 0:
        candidates = [i for i in range(1, amount) if holding[i] < largest] or [i for i in range(1, amount) if holding[i] < most]
        whole, remaining = sum([portions[i] for i in candidates]), surplus
        for i in candidates:
            more = min(most - holding[i], max(1, remaining * portions[i] // whole), surplus)
            holding[i] = holding[i] + more
            surplus = surplus - more
    return np.array(holding)


def normal_values(key, shape, deviation, limit, cuts=(), held_as=jnp.bfloat16):
    gain = block_scale(key, shape, cuts, -0.22, 0.18) if cuts else 1.0
    drawn = jax.random.normal(key, shape, jnp.float32) * deviation * gain
    return jnp.minimum(jnp.maximum(drawn, -limit), limit).astype(held_as)


def setup_inputs(seed: int = 0, part: int = 0) -> dict:
    key_of = jax.random.split(jax.random.key(seed), 6)
    part_keys = jax.random.split(jax.random.fold_in(key_of[5], part), 6)
    tokens = normal_values(part_keys[0], (TOKENS, D), 1.0, 6.0, ((0, 4), (1, 4)))
    up_weight = normal_values(key_of[1], (EXPERTS, D, FF), D ** -0.5, 0.09375, ((0, 4), (2, 4)))
    down_weight = normal_values(key_of[2], (EXPERTS, FF, D), FF ** -0.5, 0.1875, ((0, 4), (1, 4)))
    expert_ids_keys = jax.random.split(jax.random.fold_in(part_keys[3], 1), TOKENS // TOK_EXP)
    expert_ids_turns = jax.random.permutation(jax.random.fold_in(part_keys[3], 3), TOKENS // TOK_EXP)
    expert_ids = jax.vmap(lambda own, number: deal_out(jax.random.fold_in(part_keys[3], 2), own, number, TOK_EXP, EXPERTS, TOP, CAP, 2))(expert_ids_keys, expert_ids_turns).reshape((TOKENS, TOP))
    route_scores = jnp.clip(0.1 + 0.9 * jax.random.uniform(part_keys[4], (TOKENS, TOP), jnp.float32) ** block_scale(part_keys[4], (TOKENS, TOP), ((0, 4),), -0.2, 0.2), 0.1, 1.0)
    return dict(tokens=tokens, up_weight=up_weight, down_weight=down_weight, expert_ids=expert_ids, route_scores=route_scores)


def reference(tokens, up_weight, down_weight, expert_ids, route_scores):
    gate_weight = 2.5 * route_scores / jnp.sum(route_scores, axis=1, keepdims=True)
    expert_iota = jnp.arange(EXPERTS, dtype=jnp.int32)
    chosen = jnp.sum((expert_ids[:, :, None] == expert_iota[None, None, :]).astype(jnp.int32), axis=1)
    blocked = chosen.reshape(N_EXPERT, TOK_EXP, EXPERTS)
    before = (jnp.cumsum(blocked, axis=1) - blocked).reshape(TOKENS, EXPERTS)
    position = jnp.take_along_axis(before, expert_ids, axis=1)
    block_of = (jnp.arange(TOKENS, dtype=jnp.int32) // TOK_EXP)[:, None]
    slot_index = (block_of * CAP + position).astype(jnp.int32)
    token_index = jnp.broadcast_to(jnp.arange(TOKENS, dtype=jnp.int32)[:, None], expert_ids.shape)
    slot_table = jnp.full((EXPERTS, N_EXPERT * CAP), -1, jnp.int32)
    slot_table = slot_table.at[expert_ids, slot_index].set(token_index)

    def one_expert(operands):
        row_index, w_in, w_out = operands
        filled = row_index >= 0
        gathered = jnp.take(tokens, jnp.maximum(row_index, 0), axis=0)
        gathered = jnp.where(filled[:, None], gathered, jnp.zeros_like(gathered))
        projected = jnp.dot(gathered, w_in, preferred_element_type=jnp.float32)
        hidden = jax.nn.silu(projected).astype(jnp.bfloat16)
        summed = jnp.zeros((gathered.shape[0], D), jnp.float32)
        for block_index in range(N_HELPER):
            lower = block_index * FF_DEV
            partial_value = jnp.dot(hidden[:, lower:lower + FF_DEV], w_out[lower:lower + FF_DEV],
                              preferred_element_type=jnp.float32).astype(jnp.bfloat16)
            partial_value = lax.optimization_barrier(partial_value)
            summed = summed + partial_value.astype(jnp.float32)
        return summed.astype(jnp.bfloat16)

    results = lax.map(one_expert, (slot_table, up_weight, down_weight))
    picked = results[expert_ids, slot_index]
    layer_out = jnp.sum(gate_weight[:, :, None] * picked.astype(jnp.float32), axis=1)
    return layer_out.astype(jnp.bfloat16)
```

```python
import jax
import jax.numpy as jnp
from jax import lax
from jax.sharding import PartitionSpec as P


def local(tokens, up_weight, down_weight, expert_ids, route_scores):
    expert_ranks = lax.axis_size("expert")
    local_count = up_weight.shape[0]
    all_experts = local_count * expert_ranks
    gate_weight = 2.5 * route_scores / jnp.sum(route_scores, axis=1, keepdims=True)
    expert_iota = jnp.arange(all_experts, dtype=jnp.int32)
    table = jnp.sum(
        jnp.where(expert_ids[:, :, None] == expert_iota, gate_weight[:, :, None], 0.0), axis=1
    )
    full = lax.all_gather(tokens, "expert", axis=0, tiled=True)
    full = lax.all_gather(full, "helper", axis=1, tiled=True)
    share = lax.all_to_all(
        table.reshape(-1, expert_ranks, local_count).transpose(1, 0, 2),
        "expert", split_axis=0, concat_axis=0, tiled=True,
    ).reshape(-1, local_count)
    projected = jnp.einsum("td,edf->etf", full, up_weight, preferred_element_type=jnp.float32)
    hidden = (jax.nn.silu(projected) * share.T[:, :, None]).astype(jnp.bfloat16)
    total = jnp.einsum("etf,efd->td", hidden, down_weight, preferred_element_type=jnp.float32)
    total = lax.psum_scatter(total.astype(jnp.bfloat16), "helper", scatter_dimension=1, tiled=True)
    return lax.psum_scatter(total, "expert", scatter_dimension=0, tiled=True)


def solution(mesh):
    return jax.shard_map(
        local,
        mesh=mesh,
        in_specs=(
            P(("groups", "expert"), "helper"),
            P("expert", None, "helper"),
            P("expert", "helper", None),
            P(("groups", "expert"), None),
            P(("groups", "expert"), None),
        ),
        out_specs=P(("groups", "expert"), "helper"),
        check_vma=False,
    )
```

```python
import functools

import jax
import jax.numpy as jnp
from jax import lax
from jax.experimental import pallas as pl
from jax.experimental.pallas import tpu as pltpu
from jax.sharding import PartitionSpec as P

TILE = 256
LANES = 128
MESH = pl.DeviceIdType.MESH


def spread(tokens, up_weight, down_weight, expert_ids, route_scores):
    expert_ranks = lax.axis_size("expert")
    local_count = up_weight.shape[0]
    all_experts = local_count * expert_ranks
    gate_weight = 2.5 * route_scores / jnp.sum(route_scores, axis=1, keepdims=True)
    expert_iota = jnp.arange(all_experts, dtype=jnp.int32)
    table = jnp.sum(
        jnp.where(expert_ids[:, :, None] == expert_iota, gate_weight[:, :, None], 0.0), axis=1
    )
    full = lax.all_gather(tokens, "expert", axis=0, tiled=True)
    full = lax.all_gather(full, "helper", axis=1, tiled=True)
    share = lax.all_to_all(
        table.reshape(-1, expert_ranks, local_count).transpose(1, 0, 2),
        "expert", split_axis=0, concat_axis=0, tiled=True,
    ).reshape(-1, local_count)
    projected = jnp.einsum("td,edf->etf", full, up_weight, preferred_element_type=jnp.float32)
    hidden = (jax.nn.silu(projected) * share.T[:, :, None]).astype(jnp.bfloat16)
    total = jnp.einsum("etf,efd->td", hidden, down_weight, preferred_element_type=jnp.float32)
    total = lax.psum_scatter(total.astype(jnp.bfloat16), "helper", scatter_dimension=1, tiled=True)
    return lax.psum_scatter(total, "expert", scatter_dimension=0, tiled=True)


def fused_kernel(
    ranks, tokens, ids, scores, up, down, out,
    weights, near, far, gates, tables, acc, hidden, sums_far, sums_near,
    got_far, pass_far, got_x, got_near, pass_z, got_z,
    weight_sem, z_send, z_recv, g_send, g_recv, c_send, c_recv, x_send, x_recv,
    f_send, f_recv, p_send, p_recv, r_send, r_recv,
):
    rows, width = tokens.shape
    experts, ktiles = up.shape[0], up.shape[1] // 2
    chunks = ktiles
    group = experts * ktiles
    me = lax.axis_index("expert")
    helper = lax.axis_index("helper")
    core, chip = lax.rem(helper, 2), helper // 2
    core_peer = {"helper": chip * 2 + 1 - core}
    chip_peer = {"helper": (1 - chip) * 2 + core}
    columns = pl.ds(pl.multiple_of(core * width, LANES), width)
    other_columns = pl.ds(pl.multiple_of((1 - core) * width, LANES), width)

    def rank_at(step):
        return lax.rem(me + step, ranks)

    def rows_of(rank):
        return pl.ds(pl.multiple_of(rank * rows, rows), rows)

    def load_up(part, e):
        half = chip if part == 0 else 1 - chip
        return pltpu.make_async_copy(
            up.at[e, pl.ds(half * ktiles, ktiles)],
            weights.at[pl.ds(part * group + e * ktiles, ktiles)],
            weight_sem.at[part * experts + e],
        )

    def chunk_at(i):
        return jnp.where(core == 1, i, chunks - 1 - i)

    def load_down(part, i):
        half = 1 - chip if part == 0 else chip
        first = 2 * group if part == 0 else 0
        column = pl.multiple_of((half * chunks + chunk_at(i)) * TILE, TILE)
        return pltpu.make_async_copy(
            down.at[:, :, pl.ds(column, TILE)],
            weights.at[pl.ds(first + i * experts, experts)],
            weight_sem.at[2 * experts + part * chunks + i],
        )

    def remote(src, dst, send, recv, device):
        return pltpu.make_async_remote_copy(
            src_ref=src, dst_ref=dst, send_sem=send, recv_sem=recv,
            device_id=device, device_id_type=MESH,
        )

    def each(count, body):
        lax.fori_loop(0, count, lambda i, c: (body(i), c)[1], 0)

    barrier = pltpu.get_barrier_semaphore()
    for step in range(1, ranks):
        pl.semaphore_signal(barrier, inc=1, device_id={"expert": rank_at(step)}, device_id_type=MESH)
    pl.semaphore_signal(barrier, inc=1, device_id=core_peer, device_id_type=MESH)
    pl.semaphore_signal(barrier, inc=1, device_id=chip_peer, device_id_type=MESH)
    each(experts, lambda e: load_up(0, e).start())
    near[rows_of(me), columns] = tokens[...]
    score = scores[...]
    gate = 2.5 * score / jnp.sum(score, axis=1, keepdims=True)
    named = ids[...]
    lane = lax.broadcasted_iota(jnp.int32, (rows, LANES), 1)
    for step in range(ranks):
        base = rank_at(step) * experts
        total = jnp.zeros((rows, LANES), jnp.float32)
        for k in range(named.shape[1]):
            hit = named[:, k:k + 1] - base == lane
            total = total + jnp.where(hit, gate[:, k:k + 1], 0.0)
        if step == 0:
            gates[rows_of(me), :] = total
        else:
            tables[step - 1] = total
    pl.semaphore_wait(barrier, ranks + 1)

    def z_copy(step):
        here = near.at[rows_of(me), columns]
        return remote(here, here, z_send.at[step - 1], z_recv.at[step - 1], {"expert": rank_at(step)})

    def z_wait(step):
        there = near.at[rows_of(rank_at(ranks - step)), columns]
        remote(there, there, z_send.at[step - 1], z_recv.at[step - 1], {"expert": rank_at(step)}).wait_recv()

    def g_copy(step):
        return remote(
            tables.at[step - 1], gates.at[rows_of(me), :],
            g_send.at[step - 1], g_recv.at[step - 1], {"expert": rank_at(step)},
        )

    def c_copy(step):
        place = near.at[rows_of(rank_at(ranks - step)), columns]
        return remote(place, place, c_send.at[step], c_recv.at[step], core_peer)

    def x_copy(step):
        place = rows_of(rank_at(ranks - step))
        return remote(near.at[place, columns], far.at[place, columns], x_send.at[step], x_recv.at[step], chip_peer)

    def f_copy(step):
        place = far.at[rows_of(rank_at(ranks - step)), columns]
        return remote(place, place, f_send.at[step], f_recv.at[step], core_peer)

    for step in range(1, ranks):
        z_copy(step).start()
    x_copy(0).start()
    c_copy(0).start()
    for step in range(1, ranks):
        g_copy(step).start()
    each(experts, lambda e: load_up(1, e).start())
    each(chunks, lambda i: load_down(0, i).start())
    for step in range(1, ranks):
        z_wait(step)
        x_copy(step).start()
        c_copy(step).start()
    for step in range(ranks):
        place = near.at[rows_of(rank_at(ranks - step)), other_columns]
        remote(place, place, c_send.at[step], c_recv.at[step], core_peer).wait_recv()

    def product(part, e):
        lhs = near if part == 0 else far
        block = weights[pl.ds(part * group + e * ktiles, ktiles)]
        return jnp.dot(
            lhs[...], block.reshape(ktiles * TILE, TILE), preferred_element_type=jnp.float32
        )

    def first_half(e):
        load_up(0, e).wait()
        acc[e] = product(0, e)

    early = experts // 2
    each(early, first_half)
    for step in range(ranks):
        x_copy(step).wait_recv()
        f_copy(step).start()
    each(experts - early, lambda e: first_half(e + early))
    each(chunks, lambda i: load_down(1, i).start())
    for step in range(1, ranks):
        there = gates.at[rows_of(rank_at(ranks - step)), :]
        remote(there, there, g_send.at[step - 1], g_recv.at[step - 1], {"expert": rank_at(step)}).wait_recv()
    for step in range(ranks):
        place = far.at[rows_of(rank_at(ranks - step)), other_columns]
        remote(place, place, f_send.at[step], f_recv.at[step], core_peer).wait_recv()

    lane_all = lax.broadcasted_iota(jnp.int32, gates.shape, 1)

    def second_half(e):
        load_up(1, e).wait()
        value = acc[e] + product(1, e)
        share = jnp.sum(jnp.where(lane_all == e, gates[...], 0.0), axis=1, keepdims=True)
        value = value / (1.0 + jnp.exp(-value)) * share
        hidden[:, pl.ds(pl.multiple_of(e * TILE, TILE), TILE)] = value.astype(jnp.bfloat16)

    each(experts, second_half)

    def down_chunk(part, i):
        load_down(part, i).wait()
        first = 2 * group if part == 0 else 0
        block = weights[pl.ds(first + i * experts, experts)]
        value = jnp.dot(
            hidden[...], block.reshape(experts * TILE, TILE), preferred_element_type=jnp.float32
        )
        target = sums_far if part == 0 else sums_near
        target[:, pl.ds(pl.multiple_of(chunk_at(i) * TILE, TILE), TILE)] = value.astype(jnp.bfloat16)

    front = (chunks + 1) // 2
    far_pair = remote(sums_far.at[:, other_columns], got_far, p_send.at[0], p_recv.at[0], core_peer)
    near_pair = remote(sums_near.at[:, other_columns], got_near, p_send.at[1], p_recv.at[1], core_peer)
    across = remote(pass_far, got_x, p_send.at[2], p_recv.at[2], chip_peer)
    each(front, lambda i: down_chunk(0, i))
    far_pair.start()
    each(chunks - front, lambda i: down_chunk(0, i + front))
    far_pair.wait_recv()
    pass_far[...] = (
        sums_far[:, columns].astype(jnp.float32) + got_far[...].astype(jnp.float32)
    ).astype(jnp.bfloat16)
    across.start()
    each(front, lambda i: down_chunk(1, i))
    near_pair.start()
    each(chunks - front, lambda i: down_chunk(1, i + front))
    near_pair.wait_recv()
    across.wait_recv()
    pass_z[...] = (
        sums_near[:, columns].astype(jnp.float32)
        + got_near[...].astype(jnp.float32)
        + got_x[...].astype(jnp.float32)
    ).astype(jnp.bfloat16)

    def r_copy(step):
        return remote(
            pass_z.at[rows_of(rank_at(step)), :], got_z.at[step - 1],
            r_send.at[step - 1], r_recv.at[step - 1], {"expert": rank_at(step)},
        )

    for step in range(1, ranks):
        r_copy(step).start()
    total = pass_z[rows_of(me), :].astype(jnp.float32)
    for step in range(1, ranks):
        r_copy(step).wait_recv()
        total = total + got_z[step - 1].astype(jnp.float32)
    out[...] = total.astype(out.dtype)
    for step in range(1, ranks):
        z_copy(step).wait_send()
        g_copy(step).wait_send()
        r_copy(step).wait_send()
    for step in range(ranks):
        c_copy(step).wait_send()
        x_copy(step).wait_send()
        f_copy(step).wait_send()
    far_pair.wait_send()
    near_pair.wait_send()
    across.wait_send()


def fused(tokens, up_weight, down_weight, expert_ids, route_scores):
    ranks = lax.axis_size("expert")
    rows, width = tokens.shape
    experts, depth, inner = up_weight.shape
    ktiles = depth // (2 * TILE)
    every = rows * ranks
    bf16, f32 = jnp.bfloat16, jnp.float32
    vmem = pl.BlockSpec(memory_space=pltpu.VMEM)
    hbm = pl.BlockSpec(memory_space=pl.ANY)
    dma = pltpu.SemaphoreType.DMA
    return pl.pallas_call(
        functools.partial(fused_kernel, ranks),
        out_shape=jax.ShapeDtypeStruct((rows, width), bf16),
        in_specs=[vmem, vmem, vmem, hbm, hbm],
        out_specs=vmem,
        scratch_shapes=[
            pltpu.VMEM((3 * experts * ktiles, TILE, TILE), bf16),
            pltpu.VMEM((every, 2 * width), bf16),
            pltpu.VMEM((every, 2 * width), bf16),
            pltpu.VMEM((every, LANES), f32),
            pltpu.VMEM((ranks - 1, rows, LANES), f32),
            pltpu.VMEM((experts, every, TILE), f32),
            pltpu.VMEM((every, experts * TILE), bf16),
            pltpu.VMEM((every, 2 * width), bf16),
            pltpu.VMEM((every, 2 * width), bf16),
            pltpu.VMEM((every, width), bf16),
            pltpu.VMEM((every, width), bf16),
            pltpu.VMEM((every, width), bf16),
            pltpu.VMEM((every, width), bf16),
            pltpu.VMEM((every, width), bf16),
            pltpu.VMEM((ranks - 1, rows, width), bf16),
            dma((2 * experts + 2 * ktiles,)),
            dma((ranks - 1,)), dma((ranks - 1,)),
            dma((ranks - 1,)), dma((ranks - 1,)),
            dma((ranks,)), dma((ranks,)),
            dma((ranks,)), dma((ranks,)),
            dma((ranks,)), dma((ranks,)),
            dma((3,)), dma((3,)),
            dma((ranks - 1,)), dma((ranks - 1,)),
        ],
        compiler_params=pltpu.CompilerParams(
            collective_id=0, has_side_effects=True, vmem_limit_bytes=60 * 2**20
        ),
        cost_estimate=pl.CostEstimate(
            flops=4 * every * experts * depth * inner,
            bytes_accessed=4 * experts * depth * inner,
            transcendentals=every * experts * inner,
        ),
    )(
        tokens, expert_ids, route_scores,
        up_weight.reshape(experts, depth // TILE, TILE, inner), down_weight,
    )


def local(tokens, up_weight, down_weight, expert_ids, route_scores):
    ranks, helpers = lax.axis_size("expert"), lax.axis_size("helper")
    experts, depth, inner = up_weight.shape
    small = (
        ranks * tokens.shape[0] <= 128 and helpers == 4 and experts <= 16
        and depth == 3584 and inner == TILE
    )
    run = fused if small else spread
    return run(tokens, up_weight, down_weight, expert_ids, route_scores)


def solution(mesh):
    return jax.shard_map(
        local,
        mesh=mesh,
        in_specs=(
            P(("groups", "expert"), "helper"),
            P("expert", None, "helper"),
            P("expert", "helper", None),
            P(("groups", "expert"), None),
            P(("groups", "expert"), None),
        ),
        out_specs=P(("groups", "expert"), "helper"),
        check_vma=False,
    )
```

```python
import functools

import jax
import jax.numpy as jnp
from jax import lax
from jax.experimental import pallas as pl
from jax.experimental.pallas import tpu as pltpu
from jax.sharding import PartitionSpec as P

TILE = 256
LANES = 128
PIECES = (
    (0, 0, 256), (0, 256, 256), (1, 0, 256), (1, 256, 256),
    (0, 512, 256), (0, 768, 128), (1, 512, 256), (1, 768, 128),
)
SUBS = ((0, 512), (512, 384))
MESH = pl.DeviceIdType.MESH


def spread(tokens, up_weight, down_weight, expert_ids, route_scores):
    expert_ranks = lax.axis_size("expert")
    local_count = up_weight.shape[0]
    all_experts = local_count * expert_ranks
    gate_weight = 2.5 * route_scores / jnp.sum(route_scores, axis=1, keepdims=True)
    expert_iota = jnp.arange(all_experts, dtype=jnp.int32)
    table = jnp.sum(
        jnp.where(expert_ids[:, :, None] == expert_iota, gate_weight[:, :, None], 0.0), axis=1
    )
    full = lax.all_gather(tokens, "expert", axis=0, tiled=True)
    full = lax.all_gather(full, "helper", axis=1, tiled=True)
    share = lax.all_to_all(
        table.reshape(-1, expert_ranks, local_count).transpose(1, 0, 2),
        "expert", split_axis=0, concat_axis=0, tiled=True,
    ).reshape(-1, local_count)
    projected = jnp.einsum("td,edf->etf", full, up_weight, preferred_element_type=jnp.float32)
    hidden = (jax.nn.silu(projected) * share.T[:, :, None]).astype(jnp.bfloat16)
    total = jnp.einsum("etf,efd->td", hidden, down_weight, preferred_element_type=jnp.float32)
    total = lax.psum_scatter(total.astype(jnp.bfloat16), "helper", scatter_dimension=1, tiled=True)
    return lax.psum_scatter(total, "expert", scatter_dimension=0, tiled=True)


def fused_kernel(
    ranks, tokens, ids, scores, up, down, out,
    weights, near, far, gates, tables, acc, hidden, sums_far, sums_near,
    got_far, pass_far, got_x, got_near, pass_z, got_z,
    weight_sem, z_send, z_recv, g_send, g_recv, c_send, c_recv, x_send, x_recv,
    f_send, f_recv, p_send, p_recv, r_send, r_recv,
):
    rows, width = tokens.shape
    experts, ktiles = up.shape[0], up.shape[1] // 2
    group = experts * ktiles
    me = lax.axis_index("expert")
    helper = lax.axis_index("helper")
    core, chip = lax.rem(helper, 2), helper // 2
    core_peer = {"helper": chip * 2 + 1 - core}
    chip_peer = {"helper": (1 - chip) * 2 + core}
    columns = pl.ds(pl.multiple_of(core * width, LANES), width)
    other_columns = pl.ds(pl.multiple_of((1 - core) * width, LANES), width)

    def rank_at(step):
        return lax.rem(me + step, ranks)

    def rows_of(rank):
        return pl.ds(pl.multiple_of(rank * rows, rows), rows)

    def load_up(part, e):
        half = chip if part == 0 else 1 - chip
        return pltpu.make_async_copy(
            up.at[e, pl.ds(half * ktiles, ktiles)],
            weights.at[pl.ds(part * group + e * ktiles, ktiles)],
            weight_sem.at[part * experts + e],
        )

    def piece_at(part, i):
        half = 1 - chip if part == 0 else chip
        owner = 1 - core if PIECES[i][0] == 0 else core
        return owner * width + PIECES[i][1], (half * 2 + owner) * width + PIECES[i][1]

    def load_down(part, i):
        span = PIECES[i][2]
        column = pl.multiple_of(piece_at(part, i)[1], LANES)
        return pltpu.make_async_copy(
            down.at[:, :, pl.ds(column, span)],
            weights.at[pl.ds(first_tile(part, i), experts), :, pl.ds(0, span)],
            weight_sem.at[2 * experts + part * len(PIECES) + i],
        )

    def first_tile(part, i):
        if part == 0:
            return 2 * group + i * experts
        return i * experts if (i + 1) * experts <= group else 2 * group + len(PIECES) * experts

    def remote(src, dst, send, recv, device):
        return pltpu.make_async_remote_copy(
            src_ref=src, dst_ref=dst, send_sem=send, recv_sem=recv,
            device_id=device, device_id_type=MESH,
        )

    def each(count, body):
        lax.fori_loop(0, count, lambda i, c: (body(i), c)[1], 0)

    barrier = pltpu.get_barrier_semaphore()
    for step in range(1, ranks):
        pl.semaphore_signal(barrier, inc=1, device_id={"expert": rank_at(step)}, device_id_type=MESH)
    pl.semaphore_signal(barrier, inc=1, device_id=core_peer, device_id_type=MESH)
    pl.semaphore_signal(barrier, inc=1, device_id=chip_peer, device_id_type=MESH)
    each(experts, lambda e: load_up(0, e).start())
    near[rows_of(me), columns] = tokens[...]
    score = scores[...].T
    gate = 2.5 * score / jnp.sum(score, axis=1, keepdims=True)
    named = ids[...].T
    lane = lax.broadcasted_iota(jnp.int32, (rows, LANES), 1)
    for step in range(ranks):
        base = rank_at(step) * experts
        total = jnp.zeros((rows, LANES), jnp.float32)
        for k in range(named.shape[1]):
            hit = named[:, k:k + 1] - base == lane
            total = total + jnp.where(hit, gate[:, k:k + 1], 0.0)
        if step == 0:
            gates[rows_of(me), :] = total
        else:
            tables[step - 1] = total
    pl.semaphore_wait(barrier, ranks + 1)

    def z_copy(step):
        here = near.at[rows_of(me), columns]
        return remote(here, here, z_send.at[step - 1], z_recv.at[step - 1], {"expert": rank_at(step)})

    def z_wait(step):
        there = near.at[rows_of(rank_at(ranks - step)), columns]
        remote(there, there, z_send.at[step - 1], z_recv.at[step - 1], {"expert": rank_at(step)}).wait_recv()

    def g_copy(step):
        return remote(
            tables.at[step - 1], gates.at[rows_of(me), :],
            g_send.at[step - 1], g_recv.at[step - 1], {"expert": rank_at(step)},
        )

    def c_copy(step):
        place = near.at[rows_of(rank_at(ranks - step)), columns]
        return remote(place, place, c_send.at[step], c_recv.at[step], core_peer)

    def x_copy(step):
        place = rows_of(rank_at(ranks - step))
        return remote(near.at[place, columns], far.at[place, columns], x_send.at[step], x_recv.at[step], chip_peer)

    def f_copy(step):
        place = far.at[rows_of(rank_at(ranks - step)), columns]
        return remote(place, place, f_send.at[step], f_recv.at[step], core_peer)

    for step in range(1, ranks):
        z_copy(step).start()
    x_copy(0).start()
    c_copy(0).start()
    for step in range(1, ranks):
        g_copy(step).start()
    each(experts, lambda e: load_up(1, e).start())
    for i in range(len(PIECES)):
        load_down(0, i).start()
    for step in range(1, ranks):
        z_wait(step)
        x_copy(step).start()
        c_copy(step).start()
    for step in range(ranks):
        place = near.at[rows_of(rank_at(ranks - step)), other_columns]
        remote(place, place, c_send.at[step], c_recv.at[step], core_peer).wait_recv()

    def product(part, e):
        lhs = near if part == 0 else far
        block = weights[pl.ds(part * group + e * ktiles, ktiles)]
        return jnp.dot(
            lhs[...], block.reshape(ktiles * TILE, TILE), preferred_element_type=jnp.float32
        )

    def first_half(e):
        load_up(0, e).wait()
        acc[e] = product(0, e)

    early = experts // 2
    each(early, first_half)
    for step in range(ranks):
        x_copy(step).wait_recv()
        f_copy(step).start()
    each(experts - early, lambda e: first_half(e + early))
    for i in range(len(PIECES)):
        load_down(1, i).start()
    for step in range(1, ranks):
        there = gates.at[rows_of(rank_at(ranks - step)), :]
        remote(there, there, g_send.at[step - 1], g_recv.at[step - 1], {"expert": rank_at(step)}).wait_recv()
    for step in range(ranks):
        place = far.at[rows_of(rank_at(ranks - step)), other_columns]
        remote(place, place, f_send.at[step], f_recv.at[step], core_peer).wait_recv()

    lane_all = lax.broadcasted_iota(jnp.int32, gates.shape, 1)

    def second_half(e):
        load_up(1, e).wait()
        value = acc[e] + product(1, e)
        share = jnp.sum(jnp.where(lane_all == e, gates[...], 0.0), axis=1, keepdims=True)
        value = value / (1.0 + jnp.exp(-value)) * share
        hidden[:, pl.ds(pl.multiple_of(e * TILE, TILE), TILE)] = value.astype(jnp.bfloat16)

    each(experts, second_half)

    def down_piece(part, i):
        load_down(part, i).wait()
        span = PIECES[i][2]
        block = weights[pl.ds(first_tile(part, i), experts), :, pl.ds(0, span)]
        value = jnp.dot(
            hidden[...], block.reshape(experts * TILE, span), preferred_element_type=jnp.float32
        )
        target = sums_far if part == 0 else sums_near
        place = pl.multiple_of(piece_at(part, i)[0], LANES)
        target[:, pl.ds(place, span)] = value.astype(jnp.bfloat16)

    def block_of(owner, sub):
        first, span = SUBS[sub]
        return pl.ds(pl.multiple_of(owner * width + first, LANES), span)

    def sub_of(sub):
        return pl.ds(SUBS[sub][0], SUBS[sub][1])

    def pair_copy(part, sub):
        source, sink = (sums_far, got_far) if part == 0 else (sums_near, got_near)
        k = part * 2 + sub
        return remote(
            source.at[:, block_of(1 - core, sub)], sink.at[:, sub_of(sub)],
            p_send.at[k], p_recv.at[k], core_peer,
        )

    def across(sub):
        return remote(
            pass_far.at[:, sub_of(sub)], got_x.at[:, sub_of(sub)],
            p_send.at[4 + sub], p_recv.at[4 + sub], chip_peer,
        )

    def r_copy(step, sub):
        k = (step - 1) * 2 + sub
        return remote(
            pass_z.at[rows_of(rank_at(step)), sub_of(sub)], got_z.at[step - 1, :, sub_of(sub)],
            r_send.at[k], r_recv.at[k], {"expert": rank_at(step)},
        )

    for part in range(2):
        for sub in range(2):
            down_piece(part, 4 * sub)
            down_piece(part, 4 * sub + 1)
            pair_copy(part, sub).start()
            down_piece(part, 4 * sub + 2)
            down_piece(part, 4 * sub + 3)
            pair_copy(part, sub).wait_recv()
            if part == 0:
                pass_far[:, sub_of(sub)] = (
                    sums_far[:, block_of(core, sub)].astype(jnp.float32)
                    + got_far[:, sub_of(sub)].astype(jnp.float32)
                ).astype(jnp.bfloat16)
                across(sub).start()
            else:
                across(sub).wait_recv()
                pass_z[:, sub_of(sub)] = (
                    sums_near[:, block_of(core, sub)].astype(jnp.float32)
                    + got_near[:, sub_of(sub)].astype(jnp.float32)
                    + got_x[:, sub_of(sub)].astype(jnp.float32)
                ).astype(jnp.bfloat16)
                for step in range(1, ranks):
                    r_copy(step, sub).start()
    for sub in range(2):
        total = pass_z[rows_of(me), sub_of(sub)].astype(jnp.float32)
        for step in range(1, ranks):
            r_copy(step, sub).wait_recv()
            total = total + got_z[step - 1, :, sub_of(sub)].astype(jnp.float32)
        out[:, sub_of(sub)] = total.astype(out.dtype)
    for step in range(1, ranks):
        z_copy(step).wait_send()
        g_copy(step).wait_send()
        r_copy(step, 0).wait_send()
        r_copy(step, 1).wait_send()
    for step in range(ranks):
        c_copy(step).wait_send()
        x_copy(step).wait_send()
        f_copy(step).wait_send()
    for sub in range(2):
        pair_copy(0, sub).wait_send()
        pair_copy(1, sub).wait_send()
        across(sub).wait_send()


def fused(tokens, up_weight, down_weight, expert_ids, route_scores):
    ranks = lax.axis_size("expert")
    rows, width = tokens.shape
    experts, depth, inner = up_weight.shape
    ktiles = depth // (2 * TILE)
    every = rows * ranks
    bf16, f32 = jnp.bfloat16, jnp.float32
    vmem = pl.BlockSpec(memory_space=pltpu.VMEM)
    hbm = pl.BlockSpec(memory_space=pl.ANY)
    dma = pltpu.SemaphoreType.DMA
    return pl.pallas_call(
        functools.partial(fused_kernel, ranks),
        out_shape=jax.ShapeDtypeStruct((rows, width), bf16),
        in_specs=[vmem, vmem, vmem, hbm, hbm],
        out_specs=vmem,
        scratch_shapes=[
            pltpu.VMEM((experts * (2 * ktiles + len(PIECES) + 1), TILE, TILE), bf16),
            pltpu.VMEM((every, 2 * width), bf16),
            pltpu.VMEM((every, 2 * width), bf16),
            pltpu.VMEM((every, LANES), f32),
            pltpu.VMEM((ranks - 1, rows, LANES), f32),
            pltpu.VMEM((experts, every, TILE), f32),
            pltpu.VMEM((every, experts * TILE), bf16),
            pltpu.VMEM((every, 2 * width), bf16),
            pltpu.VMEM((every, 2 * width), bf16),
            pltpu.VMEM((every, width), bf16),
            pltpu.VMEM((every, width), bf16),
            pltpu.VMEM((every, width), bf16),
            pltpu.VMEM((every, width), bf16),
            pltpu.VMEM((every, width), bf16),
            pltpu.VMEM((ranks - 1, rows, width), bf16),
            dma((2 * experts + 2 * len(PIECES),)),
            dma((ranks - 1,)), dma((ranks - 1,)),
            dma((ranks - 1,)), dma((ranks - 1,)),
            dma((ranks,)), dma((ranks,)),
            dma((ranks,)), dma((ranks,)),
            dma((ranks,)), dma((ranks,)),
            dma((6,)), dma((6,)),
            dma((2 * (ranks - 1),)), dma((2 * (ranks - 1),)),
        ],
        compiler_params=pltpu.CompilerParams(
            collective_id=0, has_side_effects=True, vmem_limit_bytes=60 * 2**20
        ),
        cost_estimate=pl.CostEstimate(
            flops=4 * every * experts * depth * inner,
            bytes_accessed=4 * experts * depth * inner,
            transcendentals=every * experts * inner,
        ),
    )(
        tokens, expert_ids.T, route_scores.T,
        up_weight.reshape(experts, depth // TILE, TILE, inner), down_weight,
    )


def local(tokens, up_weight, down_weight, expert_ids, route_scores):
    ranks, helpers = lax.axis_size("expert"), lax.axis_size("helper")
    experts, depth, inner = up_weight.shape
    small = (
        ranks * tokens.shape[0] <= 128 and helpers == 4 and experts == 16
        and tokens.shape[1] == 896 and inner == TILE
    )
    run = fused if small else spread
    return run(tokens, up_weight, down_weight, expert_ids, route_scores)


def solution(mesh):
    return jax.shard_map(
        local,
        mesh=mesh,
        in_specs=(
            P(("groups", "expert"), "helper"),
            P("expert", None, "helper"),
            P("expert", "helper", None),
            P(("groups", "expert"), None),
            P(("groups", "expert"), None),
        ),
        out_specs=P(("groups", "expert"), "helper"),
        check_vma=False,
    )
```
